128 devices in a mesh: fsdp: 128 (over y, z, x, core).
Axes of the slice: x: 4, y: 4, z: 4, core: 2. Of those that a mesh axis runs over, the one named last changes fastest.
Arguments:
- inputs: bfloat16 [16384, 2048], P('fsdp'), may hold values from -6 to 6
- w_query: bfloat16 [2048, 2048], P('fsdp'), may hold values from -0.125 to 0.125
- key_weight: bfloat16 [2048, 1024], P('fsdp'), may hold values from -0.125 to 0.125
- value_weight: bfloat16 [2048, 1024], P('fsdp'), may hold values from -0.125 to 0.125
- w_out: bfloat16 [2048, 2048], P('fsdp'), may hold values from -0.375 to 0.375
- w_gate: bfloat16 [2048, 6144], P('fsdp'), may hold values from -0.125 to 0.125
- w_up: bfloat16 [2048, 6144], P('fsdp'), may hold values from -0.125 to 0.125
- w_down: bfloat16 [6144, 2048], P('fsdp'), may hold values from -0.078125 to 0.078125
- norm_gains: bfloat16 [4352], P('fsdp'), may hold values from 0.5 to 1.5
- segments: int32 [16384], P('fsdp'), may hold values from 0 to 511, as said below
- cotangent: bfloat16 [16384, 2048], P('fsdp'), may hold values from -6 to 6
Outputs:
- output: bfloat16 [16384, 2048], P('fsdp')
- grad_inputs: float32 [16384, 2048], P('fsdp')
- grad_w_query: float32 [2048, 2048], P('fsdp')
- grad_w_key: float32 [2048, 1024], P('fsdp')
- grad_w_value: float32 [2048, 1024], P('fsdp')
- grad_w_out: float32 [2048, 2048], P('fsdp')
- grad_w_gate: float32 [2048, 6144], P('fsdp')
- grad_w_up: float32 [2048, 6144], P('fsdp')
- grad_w_down: float32 [6144, 2048], P('fsdp')
- grad_gains: float32 [4352], P('fsdp')
The draws below stay inside these ranges and needn't reach their ends.
Inputs may be any that keep to these rules, and one draw needn't show every extreme that they name: `segments`: Non-decreasing; the rows of device d (rows d * 128 onward) hold 1 to 4 whole sequences, the first numbered 4 * d and, where there are two or more, the last numbered 4 * d + 3; the first and the last device hold two or more; on one device, drawn from the seed, all 128 rows are one sequence.
All inputs are finite; a program needn't handle non-finite values.
Results may differ from the reference program's by a relative error of at most 0.014.
Values may be sent and summed in bfloat16 or wider, within the bound.
A program may use at most 512 MiB of HBM per device.

```python
import math
import jax
import jax.numpy as jnp
from jax import lax

MODEL_DIM = 2048
FF = 6144
QUERY_HEADS = 16
KEY_VALUE_HEADS = 8
HEAD_SIZE = 128
DEVICE_TOKENS = 128
MAXSEG = 4
TOKENS = 16384


def draw_segments(key, part):
    key = jax.random.fold_in(key, 11)
    devices = TOKENS // DEVICE_TOKENS
    cut_key, keep_key, whole_key = jax.random.split(key, 3)
    cuts = jax.random.randint(cut_key, (devices, MAXSEG - 1), 1, DEVICE_TOKENS)
    kept = jax.random.randint(keep_key, (devices, MAXSEG - 1), 0, 4) > 0
    whole_device = jax.random.randint(whole_key, (), 1, devices - 1)
    device_index = jnp.arange(devices, dtype=jnp.int32)
    column_index = jnp.arange(MAXSEG - 1, dtype=jnp.int32)
    edge_device = (device_index[:, None] == 0) | (device_index[:, None] == devices - 1)
    kept = kept | edge_device & (column_index[None, :] == 0)
    kept = kept & (device_index[:, None] != whole_device)
    row_index = jnp.arange(DEVICE_TOKENS, dtype=jnp.int32)
    starts = jnp.any((row_index[None, :, None] == cuts[:, None, :]) & kept[:, None, :], axis=2).astype(jnp.int32)
    counted = jnp.cumsum(starts, axis=1).astype(jnp.int32)
    total = counted[:, -1:]
    local = jnp.where((counted == total) & (total > 0), MAXSEG - 1, counted)
    numbers = device_index[:, None] * MAXSEG + local
    return numbers.reshape(TOKENS).astype(jnp.int32)


def levels(own_key, extent, cuts, least, largest):
    def one(dim, parts):
        steps = jax.random.uniform(jax.random.fold_in(jax.random.fold_in(own_key, 6), dim), (parts,), jnp.float32, least / len(cuts), largest / len(cuts))
        return jnp.repeat(jnp.exp(steps), extent[dim] // parts).reshape((-1,) + (1,) * (len(extent) - dim - 1))

    factor_of = one(*cuts[0])
    for cut in cuts[1:]:
        factor_of = factor_of * one(*cut)
    return factor_of


def centred(own_key, dims, scale, limit, pieces=(), held_as=jnp.bfloat16):
    drawn = jax.random.normal(own_key, dims, jnp.float32) * scale
    if len(pieces) > 0:
        drawn = levels(own_key, dims, pieces, -0.22, 0.18) * drawn
    return jnp.clip(drawn, min=-limit, max=limit).astype(held_as)


def setup_inputs(seed: int = 0) -> dict:
    seeds = jax.random.split(jax.random.key(seed), 12)
    inputs = centred(seeds[0], (TOKENS, MODEL_DIM), 1.0, 6.0, ((0, 128),))
    w_query = centred(seeds[1], (MODEL_DIM, QUERY_HEADS * HEAD_SIZE), MODEL_DIM ** -0.5, 0.125, ((0, 128),))
    key_weight = centred(seeds[2], (MODEL_DIM, KEY_VALUE_HEADS * HEAD_SIZE), MODEL_DIM ** -0.5, 0.125, ((0, 128),))
    value_weight = centred(seeds[3], (MODEL_DIM, KEY_VALUE_HEADS * HEAD_SIZE), MODEL_DIM ** -0.5, 0.125, ((0, 128),))
    w_out = centred(seeds[4], (QUERY_HEADS * HEAD_SIZE, MODEL_DIM), (QUERY_HEADS * HEAD_SIZE // 8) ** -0.5, 0.375, ((0, 128),))
    w_gate = centred(seeds[5], (MODEL_DIM, FF), MODEL_DIM ** -0.5, 0.125, ((0, 128),))
    w_up = centred(seeds[6], (MODEL_DIM, FF), MODEL_DIM ** -0.5, 0.125, ((0, 128),))
    w_down = centred(seeds[7], (FF, MODEL_DIM), FF ** -0.5, 0.078125, ((0, 128),))
    norm_gains = jnp.clip(1.0 + 0.1 * jax.random.normal(seeds[8], (2 * MODEL_DIM + 2 * HEAD_SIZE,), jnp.float32), 0.5, 1.5).astype(jnp.bfloat16)
    segments = draw_segments(jax.random.fold_in(seeds[11], 71), 0)
    cotangent = centred(seeds[10], (TOKENS, MODEL_DIM), 1.0, 6.0, ((0, 128),))
    return {"inputs": inputs, "w_query": w_query, "key_weight": key_weight, "value_weight": value_weight, "w_out": w_out, "w_gate": w_gate, "w_up": w_up, "w_down": w_down, "norm_gains": norm_gains, "segments": segments, "cotangent": cotangent}


@jax.custom_vjp
def narrow_float(v):
    return lax.optimization_barrier(v.astype(jnp.bfloat16)).astype(jnp.float32)

@jax.custom_vjp
def narrow_backward(v):
    return v

def low_keep(v):
    return (narrow_float(v), None)

def low_pass(kept, grad):
    return (grad,)

def back_keep(v):
    return (v, None)

def back_low(kept, grad):
    return (narrow_float(grad),)
narrow_float.defvjp(low_keep, low_pass)
narrow_backward.defvjp(back_keep, back_low)
epsilon = 1e-06
rope_base = 1000000.0
highest_precision = lax.Precision.HIGHEST

def root_mean_square_norm(vector, scale_gain):
    return vector * lax.rsqrt(lax.optimization_barrier(jnp.mean(vector * vector, axis=-1, keepdims=True)) + epsilon) * scale_gain

def positions_of(segments):
    position_index = jnp.arange(segments.shape[0], dtype=jnp.int32)
    starts = jnp.concatenate([jnp.array([True]), segments[1:] != segments[:-1]])
    begins = lax.cummax(jnp.where(starts, position_index, 0), axis=0)
    return (position_index - begins).astype(jnp.int32)

def apply_rotary(vector, token_positions):
    head_width = vector.shape[-1]
    half_dim = head_width // 2
    frequency = jnp.exp(jnp.arange(half_dim, dtype=jnp.float32) * (-2.0 * math.log(rope_base) / head_width))
    angles = token_positions.astype(jnp.float32)[:, None] * frequency[None, :]
    cosine = jnp.cos(angles)[:, None, :]
    sine_part = jnp.sin(angles)[:, None, :]
    first_half = vector[..., :half_dim]
    second_half = vector[..., half_dim:]
    return jnp.concatenate([first_half * cosine - second_half * sine_part, second_half * cosine + first_half * sine_part], axis=-1)

def masked_softmax(scores, segments):
    segment_length = segments.shape[0]
    position_index = jnp.arange(segment_length, dtype=jnp.int32)
    allowed = (segments[:, None] == segments[None, :]) & (position_index[None, :] <= position_index[:, None])
    scores = jnp.where(allowed, scores, -1e+30)
    row_max = lax.optimization_barrier(jnp.max(scores, axis=-1, keepdims=True))
    exponent = jnp.exp(scores - row_max)
    return exponent / lax.optimization_barrier(jnp.sum(exponent, axis=-1, keepdims=True))

def attend_over_block(query_rows, key_matrix_rows, value_matrix_rows, segments):
    segment_length = segments.shape[0]
    grouped = query_rows.reshape(segment_length, key_matrix_rows.shape[1], -1, query_rows.shape[-1])
    scores = jnp.einsum('qhgd,khd->hgqk', grouped, key_matrix_rows, precision=highest_precision) * query_rows.shape[-1] ** (-0.5)
    weights = narrow_float(masked_softmax(narrow_backward(scores), segments))
    attended_output = jnp.einsum('hgqk,khd->qhgd', weights, value_matrix_rows, precision=highest_precision)
    return attended_output.reshape(segment_length, -1)

def forward(inputs, w_query, key_weight, value_weight, w_out, w_gate, w_up, w_down, norm_gains, segments):
    model_width = inputs.shape[1]
    attn_gain = norm_gains[:model_width]
    mlp_gain = norm_gains[model_width:2 * model_width]
    query_gain = norm_gains[2 * model_width:2 * model_width + HEAD_SIZE]
    key_gain = norm_gains[2 * model_width + HEAD_SIZE:]
    number_of_rows = inputs.shape[0]
    token_positions = positions_of(segments)
    normalized_input = narrow_float(root_mean_square_norm(inputs, attn_gain))
    query_rows = narrow_backward(jnp.dot(normalized_input, w_query, precision=highest_precision)).reshape(number_of_rows, QUERY_HEADS, HEAD_SIZE)
    key_matrix_rows = narrow_backward(jnp.dot(normalized_input, key_weight, precision=highest_precision)).reshape(number_of_rows, KEY_VALUE_HEADS, HEAD_SIZE)
    value_matrix_rows = narrow_float(narrow_backward(jnp.dot(normalized_input, value_weight, precision=highest_precision))).reshape(number_of_rows, KEY_VALUE_HEADS, HEAD_SIZE)
    query_rows = narrow_float(apply_rotary(root_mean_square_norm(query_rows, query_gain), token_positions))
    key_matrix_rows = narrow_float(apply_rotary(root_mean_square_norm(key_matrix_rows, key_gain), token_positions))
    block_list = number_of_rows // DEVICE_TOKENS
    attended_output = lax.map(jax.checkpoint(lambda group_members: attend_over_block(*group_members)), (query_rows.reshape(block_list, DEVICE_TOKENS, QUERY_HEADS, HEAD_SIZE), key_matrix_rows.reshape(block_list, DEVICE_TOKENS, KEY_VALUE_HEADS, HEAD_SIZE), value_matrix_rows.reshape(block_list, DEVICE_TOKENS, KEY_VALUE_HEADS, HEAD_SIZE), segments.reshape(block_list, DEVICE_TOKENS)))
    attended_output = narrow_float(narrow_backward(attended_output.reshape(number_of_rows, QUERY_HEADS * HEAD_SIZE)))
    hidden_state = inputs + narrow_backward(jnp.dot(attended_output, w_out, precision=highest_precision))
    normed_two = narrow_float(root_mean_square_norm(hidden_state, mlp_gain))
    gate_part = narrow_backward(jnp.dot(normed_two, w_gate, precision=highest_precision))
    up_part = narrow_backward(jnp.dot(normed_two, w_up, precision=highest_precision))
    active = narrow_float(jax.nn.silu(gate_part) * up_part)
    return hidden_state + narrow_backward(jnp.dot(active, w_down, precision=highest_precision))

def reference(inputs, w_query, key_weight, value_weight, w_out, w_gate, w_up, w_down, norm_gains, segments, cotangent):
    floats = tuple((tensor.astype(jnp.float32) for tensor in (inputs, w_query, key_weight, value_weight, w_out, w_gate, w_up, w_down, norm_gains)))
    output, pullback = jax.vjp(lambda *tensors: forward(*tensors, segments), *floats)
    gradients = pullback(cotangent.astype(jnp.float32))
    return (output.astype(jnp.bfloat16), gradients[0], gradients[1], gradients[2], gradients[3], gradients[4], gradients[5], gradients[6], gradients[7], gradients[8])
```

```python
import math

import jax
import jax.numpy as jnp
from jax import lax
from jax.sharding import Mesh, PartitionSpec as P

QUERY_HEADS = 16
KEY_VALUE_HEADS = 8
HEAD_SIZE = 128
EPSILON = 1e-06
ROPE_BASE = 1000000.0
MODEL = ("x", "c")
TOKEN = ("y", "z")
F32 = jnp.float32
BF16 = jnp.bfloat16


def rms_scale(v):
    return lax.rsqrt(jnp.mean(v * v, axis=-1, keepdims=True) + EPSILON)


def rms_backward(v, r, e):
    return r * e - v * (r * r * r) * jnp.mean(e * v, axis=-1, keepdims=True)


def rotation_tables(segments):
    rows = segments.shape[-1]
    index = jnp.arange(rows, dtype=jnp.int32)
    same = segments[:, :, None] == segments[:, None, :]
    begin = jnp.min(jnp.where(same, index[None, None, :], rows), axis=-1)
    position = (index[None, :] - begin).astype(F32)
    half = HEAD_SIZE // 2
    frequency = jnp.exp(jnp.arange(half, dtype=F32) * (-2.0 * math.log(ROPE_BASE) / HEAD_SIZE))
    angles = position[..., None] * frequency
    return jnp.cos(angles), jnp.sin(angles), same & (index[None, None, :] <= index[None, :, None])


def rotate(u, cosine, sine):
    half = HEAD_SIZE // 2
    a, b = u[..., :half], u[..., half:]
    return jnp.concatenate([a * cosine - b * sine, b * cosine + a * sine], axis=-1)


def rotate_back(u, cosine, sine):
    return rotate(u, cosine, -sine)


def mm(a, b, contract):
    return lax.dot_general(a, b, (contract, ((), ())), preferred_element_type=F32)


def gather_model(a):
    return lax.all_gather(a, MODEL, axis=0, tiled=True)


def gather_token(a):
    return lax.all_gather(a, TOKEN, axis=0, tiled=True)


def scatter_model(a):
    return lax.psum_scatter(a, MODEL, scatter_dimension=0, tiled=True)


def scatter_token(a):
    return lax.psum_scatter(a, TOKEN, scatter_dimension=0, tiled=True)


def swap_model(a):
    return lax.all_to_all(a, MODEL, 0, 0, tiled=True)


def per_device(
    inputs, w_query, key_weight, value_weight, w_out, w_gate, w_up, w_down, norm_gains, segments, cotangent
):
    rows, width = inputs.shape
    ways = 8
    teams = 16
    group = QUERY_HEADS // KEY_VALUE_HEADS
    shard = w_query.shape[0]
    hidden_cut = w_down.shape[0]
    hidden_units = teams * hidden_cut
    tokens = rows * ways
    scale = HEAD_SIZE ** (-0.5)

    qkv_send = jnp.concatenate(
        [
            w_query.reshape(shard, ways, -1),
            key_weight.reshape(shard, ways, -1),
            value_weight.reshape(shard, ways, -1),
        ],
        axis=-1,
    ).transpose(1, 0, 2)
    gate_up_send = jnp.stack([w_gate, w_up], axis=1)
    gate_up_send = gate_up_send.reshape(shard, 2, teams, ways, hidden_cut).transpose(3, 0, 1, 2, 4)
    gate_up_send = gate_up_send.reshape(ways, shard, 2 * hidden_units)
    w_qkv = gather_token(swap_model(qkv_send).reshape(ways * shard, -1))
    gains = gather_token(gather_model(norm_gains)).astype(F32)
    attn_gain = gains[:width]
    mlp_gain = gains[width : 2 * width]
    query_gain = gains[2 * width : 2 * width + HEAD_SIZE]
    key_gain = gains[2 * width + HEAD_SIZE :]

    x = gather_model(inputs).astype(F32)
    segment_blocks = gather_model(segments).reshape(ways, rows)
    normed = (x * rms_scale(x) * attn_gain).astype(BF16)
    qkv = mm(normed, w_qkv, ((1,), (0,)))
    cosine, sine, allowed = rotation_tables(segment_blocks)
    query_pre = qkv[:, : group * HEAD_SIZE].reshape(ways, rows, group, HEAD_SIZE)
    key_pre = qkv[:, group * HEAD_SIZE : (group + 1) * HEAD_SIZE].reshape(ways, rows, HEAD_SIZE)
    value = qkv[:, (group + 1) * HEAD_SIZE :].astype(BF16).reshape(ways, rows, HEAD_SIZE)
    query_r = rms_scale(query_pre)
    key_r = rms_scale(key_pre)
    cosine_q, sine_q = cosine[:, :, None, :], sine[:, :, None, :]
    query = rotate(query_pre * query_r * query_gain, cosine_q, sine_q).astype(BF16)
    key = rotate(key_pre * key_r * key_gain, cosine, sine).astype(BF16)
    scores = jnp.einsum("bqgd,bkd->bgqk", query, key, preferred_element_type=F32) * scale
    scores = jnp.where(allowed[:, None], scores, -1e30)
    exponent = jnp.exp(scores - jnp.max(scores, axis=-1, keepdims=True))
    probs_float = exponent / jnp.sum(exponent, axis=-1, keepdims=True)
    probs = probs_float.astype(BF16)
    attended = jnp.einsum("bgqk,bkd->gdbq", probs, value, preferred_element_type=F32).astype(BF16)
    attended = attended.reshape(group, ways, -1, tokens).transpose(1, 0, 2, 3)
    attended = swap_model(attended).reshape(-1, tokens)
    out_rows = gather_token(w_out)
    hidden = inputs.astype(F32) + scatter_model(mm(attended, out_rows, ((0,), (0,))).astype(BF16)).astype(F32)

    gate_up_rows = gather_token(swap_model(gate_up_send).reshape(ways * shard, -1))
    down_rows = gather_token(w_down)
    hidden_r = rms_scale(hidden)
    normed_two = gather_model((hidden * hidden_r * mlp_gain).astype(BF16))
    dy = gather_model(cotangent)
    gate_up = mm(normed_two, gate_up_rows, ((1,), (0,)))
    gate, up = gate_up[:, :hidden_units], gate_up[:, hidden_units:]
    s = 1.0 / (1.0 + jnp.exp(-gate))
    silu = gate * s
    active = (silu * up).astype(BF16)
    out_partial = mm(active, down_rows, ((1,), (0,))).astype(BF16)
    output = (hidden + scatter_model(out_partial).astype(F32)).astype(BF16)
    d_active = mm(dy, down_rows, ((1,), (1,)))
    d_gate = (d_active * up * (s * (1.0 + gate * (1.0 - s)))).astype(BF16)
    d_up = (d_active * silu).astype(BF16)
    d_gate_up = jnp.concatenate([d_gate, d_up], axis=1)
    grad_down = mm(active, dy, ((0,), (0,)))
    grad_gate_up = mm(normed_two, d_gate_up, ((0,), (0,)))
    d_normed_two = scatter_model(mm(d_gate_up, gate_up_rows, ((1,), (1,))).astype(BF16)).astype(F32)
    d_hidden = cotangent.astype(F32) + rms_backward(hidden, hidden_r, d_normed_two * mlp_gain)
    d_mlp_gain = jnp.sum(d_normed_two * hidden * hidden_r, axis=0)

    d_hidden_low = gather_model(d_hidden.astype(BF16))
    grad_out = mm(attended, d_hidden_low, ((1,), (0,)))
    d_attended = mm(out_rows, d_hidden_low, ((1,), (1,))).astype(BF16)
    d_attended = swap_model(d_attended.reshape(ways, group, -1, tokens))
    d_attended = d_attended.transpose(1, 0, 2, 3).reshape(group, HEAD_SIZE, ways, rows)
    d_probs = jnp.einsum("gdbq,bkd->bgqk", d_attended, value, preferred_element_type=F32)
    d_value = jnp.einsum("bgqk,gdbq->bkd", probs, d_attended, preferred_element_type=F32).astype(BF16)
    d_scores = probs_float * (d_probs - jnp.sum(probs_float * d_probs, axis=-1, keepdims=True))
    d_scores = d_scores.astype(BF16)
    d_query = jnp.einsum("bgqk,bkd->bqgd", d_scores, key, preferred_element_type=F32) * scale
    d_key = jnp.einsum("bgqk,bqgd->bkd", d_scores, query, preferred_element_type=F32) * scale
    d_query = rotate_back(d_query, cosine_q, sine_q)
    d_key = rotate_back(d_key, cosine, sine)
    d_query_gain = jnp.sum(d_query * query_pre * query_r, axis=(0, 1, 2))
    d_key_gain = jnp.sum(d_key * key_pre * key_r, axis=(0, 1))
    d_query = rms_backward(query_pre, query_r, d_query * query_gain).astype(BF16)
    d_key = rms_backward(key_pre, key_r, d_key * key_gain).astype(BF16)
    d_qkv = jnp.concatenate(
        [d_query.reshape(tokens, -1), d_key.reshape(tokens, -1), d_value.reshape(tokens, -1)], axis=1
    )
    grad_qkv = mm(normed, d_qkv, ((0,), (0,)))
    d_normed = scatter_model(mm(d_qkv, w_qkv, ((1,), (1,))).astype(BF16)).astype(F32)
    own = inputs.astype(F32)
    own_r = rms_scale(own)
    grad_inputs = d_hidden + rms_backward(own, own_r, d_normed * attn_gain)
    d_attn_gain = jnp.sum(d_normed * own * own_r, axis=0)
    gain_terms = jnp.concatenate([d_attn_gain, d_mlp_gain, d_query_gain, d_key_gain])
    grad_gains = scatter_model(
        lax.psum_scatter(
            gain_terms.reshape(teams, -1), TOKEN, scatter_dimension=0, tiled=True
        ).reshape(-1)
    )

    grad_w_down = scatter_token(grad_down.astype(BF16)).astype(F32)
    grad_w_out = scatter_token(grad_out.astype(BF16)).astype(F32)
    grad_gate_up = swap_model(scatter_token(grad_gate_up.astype(BF16)).reshape(ways, shard, -1))
    grad_gate_up = grad_gate_up.reshape(ways, shard, 2, teams, hidden_cut).transpose(2, 1, 3, 0, 4)
    grad_gate_up = grad_gate_up.reshape(2, shard, -1).astype(F32)
    grad_qkv = swap_model(scatter_token(grad_qkv.astype(BF16)).reshape(ways, shard, -1))
    grad_qkv = grad_qkv.transpose(1, 0, 2).astype(F32)
    grad_w_query = grad_qkv[:, :, : group * HEAD_SIZE].reshape(shard, -1)
    grad_w_key = grad_qkv[:, :, group * HEAD_SIZE : (group + 1) * HEAD_SIZE].reshape(shard, -1)
    grad_w_value = grad_qkv[:, :, (group + 1) * HEAD_SIZE :].reshape(shard, -1)
    return (
        output,
        grad_inputs,
        grad_w_query,
        grad_w_key,
        grad_w_value,
        grad_w_out,
        grad_gate_up[0],
        grad_gate_up[1],
        grad_w_down,
        grad_gains,
    )


def solution(mesh):
    cube = Mesh(mesh.devices.reshape(4, 4, 4, 2), ("y", "z", "x", "c"))
    every = ("y", "z", "x", "c")
    matrix, vector = P(every, None), P(every)
    return jax.shard_map(
        per_device,
        mesh=cube,
        in_specs=(matrix,) * 8 + (vector, vector, matrix),
        out_specs=(matrix,) * 9 + (vector,),
        check_vma=False,
    )
```

```python
import functools
import math

import jax
import jax.numpy as jnp
from jax import lax
from jax.experimental import pallas as pl
from jax.experimental.pallas import tpu as pltpu
from jax.sharding import Mesh, PartitionSpec as P

QUERY_HEADS = 16
KEY_VALUE_HEADS = 8
HEAD_SIZE = 128
EPSILON = 1e-06
ROPE_BASE = 1000000.0
F32 = jnp.float32
BF16 = jnp.bfloat16
MESH = pl.DeviceIdType.MESH
SIZES = dict(y=4, z=4, x=4, c=2)


def rms_scale(v):
    return lax.rsqrt(jnp.mean(v * v, axis=-1, keepdims=True) + EPSILON)


def rms_backward(v, r, e):
    return r * e - v * (r * r * r) * jnp.mean(e * v, axis=-1, keepdims=True)


def rotation_tables(segments):
    rows = segments.shape[-1]
    index = jnp.arange(rows, dtype=jnp.int32)
    same = segments[:, :, None] == segments[:, None, :]
    begin = jnp.min(jnp.where(same, index[None, None, :], rows), axis=-1)
    position = (index[None, :] - begin).astype(F32)
    half = HEAD_SIZE // 2
    frequency = jnp.exp(jnp.arange(half, dtype=F32) * (-2.0 * math.log(ROPE_BASE) / HEAD_SIZE))
    angles = position[..., None] * frequency
    return jnp.cos(angles), jnp.sin(angles), same & (index[None, None, :] <= index[None, :, None])


def rotate(u, cosine, sine):
    half = HEAD_SIZE // 2
    a, b = u[..., :half], u[..., half:]
    return jnp.concatenate([a * cosine - b * sine, b * cosine + a * sine], axis=-1)


def rotate_back(u, cosine, sine):
    return rotate(u, cosine, -sine)


def mm(a, b, contract):
    return lax.dot_general(a, b, (contract, ((), ())), preferred_element_type=F32)


class Kernel:
    def __init__(self, send_sem, recv_sem, local_sem):
        self.send_sem, self.recv_sem, self.local_sem = send_sem, recv_sem, local_sem
        self.count = self.local_count = 0
        self.sent, self.kept = [], []
        self.at = {name: lax.axis_index(name) for name in ("y", "z", "x", "c")}

    def peer(self, **steps):
        return {
            name: lax.rem(self.at[name] + step % SIZES[name], SIZES[name])
            for name, step in steps.items()
        }

    def greet(self, peers):
        barrier = pltpu.get_barrier_semaphore()
        for steps in peers:
            pl.semaphore_signal(barrier, inc=1, device_id=self.peer(**steps), device_id_type=MESH)
        pl.semaphore_wait(barrier, len(peers))

    def send(self, source, target, **steps):
        copy = pltpu.make_async_remote_copy(
            src_ref=source,
            dst_ref=target,
            send_sem=self.send_sem.at[self.count],
            recv_sem=self.recv_sem.at[self.count],
            device_id=self.peer(**steps),
            device_id_type=MESH,
        )
        self.count += 1
        copy.start()
        self.sent.append(copy)
        return copy

    def local(self, source, target):
        copy = pltpu.make_async_copy(source, target, self.local_sem.at[self.local_count])
        self.local_count += 1
        copy.start()
        return copy

    def drain(self):
        for copy in self.sent:
            copy.wait_send()


GROUP_PEERS = [dict(x=dx, c=dc) for dx in range(4) for dc in range(2) if dx or dc]
RING_PEERS = [dict(y=1), dict(y=-1), dict(z=1), dict(z=-1)]
FAR_PEERS = RING_PEERS + [dict(y=2), dict(z=2)]


def round_robin(tasks):
    tasks = list(tasks)
    while tasks:
        for task in list(tasks):
            try:
                next(task)
            except StopIteration:
                tasks.remove(task)


def halves(cut, axis=-2):
    low, size = cut
    half = size // 2

    def view(start):
        def take(ref):
            index = [slice(None)] * len(ref.shape)
            index[axis] = pl.ds(start, half)
            return ref.at[tuple(index)]

        return take

    return view(low), view(low + half)


def part_of(cut, axis):
    low, size = cut

    def take(ref):
        index = [slice(None)] * len(ref.shape)
        index[axis] = pl.ds(low, size)
        return ref.at[tuple(index)]

    return take


def ring_gather(k, axis, block, cut, cut_axis):
    first, second = halves(cut, cut_axis)
    me = k.at[axis]
    after, before = lax.rem(me + 1, 4), lax.rem(me + 3, 4)
    up, down = {axis: 1}, {axis: -1}
    own = block(me)
    c1 = k.send(first(own), first(own), **up)
    c2 = k.send(second(own), second(own), **down)
    c3 = k.send(second(own), second(own), **up)
    c4 = k.send(first(own), first(own), **down)
    yield
    c1.wait_recv()
    f1 = k.send(first(block(before)), first(block(before)), **up)
    c2.wait_recv()
    f2 = k.send(second(block(after)), second(block(after)), **down)
    yield
    c3.wait_recv()
    c4.wait_recv()
    f1.wait_recv()
    f2.wait_recv()


def gather_planes(k, whole, extent, cut_axis):
    half = extent // 2
    low, high = (0, half), (half, half)
    y, z = k.at["y"], k.at["z"]

    def one():
        yield from ring_gather(k, "z", lambda i: whole.at[y, i], low, cut_axis)
        yield from ring_gather(k, "y", lambda i: whole.at[i], low, cut_axis)

    def two():
        yield from ring_gather(k, "y", lambda i: whole.at[i, z], high, cut_axis)
        yield from ring_gather(k, "z", lambda i: whole.at[:, i], high, cut_axis)

    tasks = [one(), two()]
    while tasks:
        for task in list(tasks):
            try:
                next(task)
            except StopIteration:
                tasks.remove(task)
        yield


def add_rows(target, sources, rows=16):
    shape = target.shape
    leads = [()]
    for extent in shape[:-2]:
        leads = [lead + (i,) for lead in leads for i in range(extent)]

    def step(i, carry):
        span = pl.ds(pl.multiple_of(i * rows, rows), rows)
        for lead in leads:
            total = sources[0][lead + (span,)].astype(F32)
            for source in sources[1:]:
                total = total + source[lead + (span,)].astype(F32)
            target[lead + (span,)] = total.astype(target.dtype)
        return carry

    lax.fori_loop(0, shape[-2] // rows, step, 0)


def ring_reduce(k, axis, block, cut, cut_axis, near, far, target):
    first, second = halves(cut, cut_axis)
    near_first, near_second = halves((0, cut[1]), cut_axis)
    take = part_of(cut, cut_axis)
    me = k.at[axis]
    after, before, across = lax.rem(me + 1, 4), lax.rem(me + 3, 4), lax.rem(me + 2, 4)
    up, down = {axis: 1}, {axis: -1}
    c1 = k.send(first(block(across)), far[0], **up)
    c2 = k.send(second(block(across)), far[1], **down)
    c3 = k.send(second(block(after)), near_second(near[0]), **up)
    c4 = k.send(first(block(before)), near_first(near[1]), **down)
    yield
    c1.wait_recv()
    add_rows(first(block(after)), [first(block(after)), far[0]])
    c5 = k.send(first(block(after)), near_first(near[0]), **up)
    c2.wait_recv()
    add_rows(second(block(before)), [second(block(before)), far[1]])
    c6 = k.send(second(block(before)), near_second(near[1]), **down)
    yield
    for copy in (c3, c4, c5, c6):
        copy.wait_recv()
    add_rows(target, [take(block(me)), near[0], near[1]])


def reduce_planes(k, whole, extent, cut_axis, room, target):
    half = extent // 2
    low, high = (0, half), (half, half)
    y, z = k.at["y"], k.at["z"]
    low_part, high_part = part_of(low, cut_axis), part_of(high, cut_axis)

    def one():
        yield from ring_reduce(
            k, "z", lambda i: whole.at[:, i], low, cut_axis, *room[0], low_part(whole.at[:, z])
        )
        yield from ring_reduce(
            k, "y", lambda i: whole.at[i, z], low, cut_axis, *room[1], low_part(target)
        )

    def two():
        yield from ring_reduce(
            k, "y", lambda i: whole.at[i], high, cut_axis, *room[2], high_part(whole.at[y])
        )
        yield from ring_reduce(
            k, "z", lambda i: whole.at[y, i], high, cut_axis, *room[3], high_part(target)
        )

    tasks = [one(), two()]
    while tasks:
        for task in list(tasks):
            try:
                next(task)
            except StopIteration:
                tasks.remove(task)
        yield


def reduce_room(shape, cut_axis):
    def ranges(parts):
        cut = list(shape)
        cut[cut_axis] //= parts
        return tuple(cut)

    shapes = []
    for lead in ((4,), (), (4,), ()):
        shapes.append(
            (
                [pltpu.VMEM(lead + ranges(2), BF16)] * 2,
                [pltpu.VMEM(lead + ranges(4), BF16)] * 2,
            )
        )
    return shapes


def gather_group(k, own, whole):
    x, c = k.at["x"], k.at["c"]
    first, second = halves((0, own.shape[-2]))
    after, before, across = lax.rem(x + 1, 4), lax.rem(x + 3, 4), lax.rem(x + 2, 4)
    up, down, other = dict(x=1), dict(x=-1), dict(c=1)

    def block(i):
        return whole.at[2 * i + c]

    mine = block(x)
    c1 = k.send(first(own), first(mine), **up)
    c2 = k.send(second(own), second(mine), **down)
    c3 = k.send(second(own), second(mine), **up)
    c4 = k.send(first(own), first(mine), **down)
    pair = [k.send(own, mine, **other)]
    kept = k.local(own, mine)
    yield
    c1.wait_recv()
    f1 = k.send(first(block(before)), first(block(before)), **up)
    c2.wait_recv()
    f2 = k.send(second(block(after)), second(block(after)), **down)
    pair.append(k.send(first(block(before)), first(block(before)), **other))
    pair.append(k.send(second(block(after)), second(block(after)), **other))
    yield
    c3.wait_recv()
    pair.append(k.send(second(block(before)), second(block(before)), **other))
    c4.wait_recv()
    pair.append(k.send(first(block(after)), first(block(after)), **other))
    yield
    f1.wait_recv()
    pair.append(k.send(first(block(across)), first(block(across)), **other))
    f2.wait_recv()
    pair.append(k.send(second(block(across)), second(block(across)), **other))
    yield
    for copy in pair:
        copy.wait_recv()
    kept.wait()


def group_room(rows, columns):
    return [
        pltpu.VMEM((4, rows, columns), BF16),
        pltpu.VMEM((rows, columns), BF16),
        pltpu.VMEM((rows, columns), BF16),
        pltpu.VMEM((rows // 2, columns), BF16),
        pltpu.VMEM((rows // 2, columns), BF16),
    ]


def reduce_group(k, terms, room, finish):
    pair, from_before, from_after, far_up, far_down = room
    x, c = k.at["x"], k.at["c"]
    first, second = halves((0, terms.shape[-2]))
    after, before, across = lax.rem(x + 1, 4), lax.rem(x + 3, 4), lax.rem(x + 2, 4)
    up, down, other = dict(x=1), dict(x=-1), dict(c=1)

    def block(i):
        return terms.at[2 * i + c]

    def lent(i):
        return terms.at[2 * i + 1 - c]

    p1 = k.send(first(lent(across)), first(pair.at[across]), **other)
    p2 = k.send(second(lent(across)), second(pair.at[across]), **other)
    p3 = k.send(lent(after), pair.at[after], **other)
    p4 = k.send(lent(before), pair.at[before], **other)
    p5 = k.send(lent(x), pair.at[x], **other)
    p1.wait_recv()
    add_rows(first(block(across)), [first(block(across)), first(pair.at[across])])
    c1 = k.send(first(block(across)), far_up, **up)
    p2.wait_recv()
    add_rows(second(block(across)), [second(block(across)), second(pair.at[across])])
    c2 = k.send(second(block(across)), far_down, **down)
    p3.wait_recv()
    add_rows(second(block(after)), [second(block(after)), second(pair.at[after])])
    c3 = k.send(second(block(after)), second(from_before), **up)
    p4.wait_recv()
    add_rows(first(block(before)), [first(block(before)), first(pair.at[before])])
    c4 = k.send(first(block(before)), first(from_after), **down)
    yield
    c1.wait_recv()
    add_rows(first(block(after)), [first(block(after)), first(pair.at[after]), far_up])
    c5 = k.send(first(block(after)), first(from_before), **up)
    c2.wait_recv()
    add_rows(second(block(before)), [second(block(before)), second(pair.at[before]), far_down])
    c6 = k.send(second(block(before)), second(from_after), **down)
    yield
    for copy in (p5, c3, c4, c5, c6):
        copy.wait_recv()
    finish([block(x), pair.at[x], from_before, from_after])


def swap_group(k, terms, taken):
    x, c = k.at["x"], k.at["c"]
    me = 2 * x + c
    kept = k.local(terms.at[me], taken.at[me])
    copies = []
    for steps in GROUP_PEERS:
        there = k.peer(**steps)
        copies.append(k.send(terms.at[2 * there["x"] + there["c"]], taken.at[me], **steps))
    yield
    for copy in copies:
        copy.wait_recv()
    kept.wait()


def spread_group(k, own, whole):
    me = 2 * k.at["x"] + k.at["c"]
    kept = k.local(own, whole.at[me])
    copies = [k.send(own, whole.at[me], **steps) for steps in GROUP_PEERS]
    yield
    for copy in copies:
        copy.wait_recv()
    kept.wait()


def spread_ring(k, axis, block):
    own = block(k.at[axis])
    copies = [k.send(own, own, **{axis: step}) for step in (1, 2, 3)]
    yield
    for copy in copies:
        copy.wait_recv()


def sum_ring(k, axis, block, room, target):
    me = k.at[axis]
    copies = [
        k.send(block(lax.rem(me + step, 4)), room.at[step - 1], **{axis: step}) for step in (1, 2, 3)
    ]
    yield
    for copy in copies:
        copy.wait_recv()
    target[...] = ((block(me)[...] + room[0]) + room[1]) + room[2]


def communicate(body, arrays, outs, room, peers, ident, copies, moved, in_vmem=()):
    def kernel(*refs):
        ins, rest = refs[: len(arrays)], refs[len(arrays) :]
        given, rest = rest[: len(outs)], rest[len(outs) :]
        k = Kernel(*rest[1:])
        k.greet(peers)
        body(k, ins, given, rest[0])
        k.drain()

    vmem, any_place = pl.BlockSpec(memory_space=pltpu.VMEM), pl.BlockSpec(memory_space=pl.ANY)
    return pl.pallas_call(
        kernel,
        out_shape=[jax.ShapeDtypeStruct(shape, kind) for shape, kind, _ in outs],
        in_specs=[vmem if i in in_vmem else any_place for i in range(len(arrays))],
        out_specs=[vmem if held else any_place for _, _, held in outs],
        scratch_shapes=[
            room,
            pltpu.SemaphoreType.DMA((copies,)),
            pltpu.SemaphoreType.DMA((copies,)),
            pltpu.SemaphoreType.DMA((8,)),
        ],
        compiler_params=pltpu.CompilerParams(
            collective_id=ident, has_side_effects=True, vmem_limit_bytes=56 * 1024 * 1024
        ),
        cost_estimate=pl.CostEstimate(flops=0, bytes_accessed=moved, transcendentals=0),
    )(*arrays)


def first_exchange(x, segments, gains, qkv, gate_up, w_out):
    def body(k, ins, outs, room):
        x, segments, gains, qkv, gate_up, w_out = ins
        x_all, segments_all, gains_all, qkv_all, gate_up_own, w_out_all = outs
        y, z = k.at["y"], k.at["z"]
        kept = k.local(w_out, w_out_all.at[y, z])

        def weights():
            yield from swap_group(k, qkv, qkv_all.at[y, z])
            yield from gather_planes(k, qkv_all, 8, -3)

        def small():
            yield from spread_group(k, gains, gains_all.at[y, z])
            yield from spread_ring(k, "z", lambda i: gains_all.at[y, i])
            yield from spread_ring(k, "y", lambda i: gains_all.at[i])

        def more():
            kept.wait()
            yield from gather_planes(k, w_out_all, w_out.shape[-1], -1)

        round_robin([
            weights(),
            small(),
            spread_group(k, segments, segments_all),
            gather_group(k, x, x_all),
            more(),
            swap_group(k, gate_up, gate_up_own),
        ])

    rows, width = x.shape
    return communicate(
        body,
        [x, segments, gains, qkv, gate_up, w_out],
        [
            ((8, rows, width), BF16, False),
            ((8,) + segments.shape, jnp.int32, False),
            ((4, 4, 8) + gains.shape, F32, False),
            ((4, 4) + qkv.shape, BF16, False),
            (gate_up.shape, BF16, False),
            ((4, 4) + w_out.shape, BF16, False),
        ],
        [],
        GROUP_PEERS + FAR_PEERS,
        1,
        128,
        8 * rows * width * 4,
    )


def swap_call(ident, *arrays):
    def body(k, ins, outs, room):
        round_robin([swap_group(k, a, b) for a, b in zip(ins, outs)])

    return communicate(
        body, list(arrays), [(a.shape, a.dtype, False) for a in arrays], [], GROUP_PEERS, ident, 32, 1 << 20
    )


def sum_and_gather(ident, terms, own, cut_axis):
    def body(k, ins, outs, room):
        terms, own = ins
        total, whole = outs
        kept = k.local(own, whole.at[k.at["y"], k.at["z"]])

        def finish(parts):
            add_rows(total, parts)

        def gather():
            kept.wait()
            yield from gather_planes(k, whole, own.shape[cut_axis], cut_axis)

        round_robin([gather(), reduce_group(k, terms, room, finish)])

    return communicate(
        body,
        [terms, own],
        [(terms.shape[1:], F32, True), ((4, 4) + own.shape, BF16, False)],
        group_room(*terms.shape[1:]),
        GROUP_PEERS + RING_PEERS,
        ident,
        64,
        1 << 24,
        (0,),
    )


def gather_both(ident, rows_own, own, cut_axis):
    def body(k, ins, outs, room):
        own = ins[-1]
        whole = outs[-1]
        kept = k.local(own, whole.at[k.at["y"], k.at["z"]])

        def gather():
            kept.wait()
            yield from gather_planes(k, whole, own.shape[cut_axis], cut_axis)

        def groups():
            for a, b in zip(ins[:-1], outs[:-1]):
                yield from gather_group(k, a, b)

        round_robin([gather(), groups()])

    return communicate(
        body,
        list(rows_own) + [own],
        [((8,) + a.shape, BF16, False) for a in rows_own] + [((4, 4) + own.shape, BF16, False)],
        [],
        GROUP_PEERS + RING_PEERS,
        ident,
        80,
        1 << 24,
    )


def sum_both(ident, terms, planes, cut_axes, gather=None):
    groups, sums = len(terms), len(planes)

    def body(k, ins, outs, room):
        def on_group():
            for i in range(groups):
                def finish(parts, i=i):
                    add_rows(outs[i], parts)

                yield from reduce_group(k, ins[i], room[i], finish)
            if gather is not None:
                yield from gather_group(k, ins[-1], outs[-1])

        def on_planes():
            for i in range(groups, groups + sums):
                yield from reduce_planes(
                    k, ins[i], ins[i].shape[cut_axes[i - groups]], cut_axes[i - groups], room[i], outs[i]
                )

        round_robin([on_planes(), on_group()])

    extra = [] if gather is None else [gather]
    return communicate(
        body,
        list(terms) + list(planes) + extra,
        [(a.shape[1:], F32, True) for a in terms]
        + [(a.shape[2:], BF16, True) for a in planes]
        + [((8,) + a.shape, BF16, False) for a in extra],
        [group_room(*a.shape[1:]) for a in terms]
        + [reduce_room(a.shape[2:], cut) for a, cut in zip(planes, cut_axes)],
        GROUP_PEERS + RING_PEERS,
        ident,
        128,
        1 << 24,
        tuple(range(groups + sums)),
    )


def last_exchange(gate_up, qkv, gains):
    def body(k, ins, outs, room):
        gate_up, qkv, gains = ins
        gate_up_own, qkv_own, gains_own = outs
        y, z = k.at["y"], k.at["z"]

        def small():
            yield from swap_group(k, gains, room[0])
            part = room[0][0]
            for i in range(1, 8):
                part = part + room[0][i]
            room[1][...] = part
            yield from sum_ring(k, "z", lambda i: room[1].at[:, i], room[2], room[3])
            yield from sum_ring(k, "y", lambda i: room[3].at[i], room[4], gains_own)

        round_robin([small(), swap_group(k, gate_up, gate_up_own), swap_group(k, qkv, qkv_own)])

    lanes = gains.shape[3:]
    return communicate(
        body,
        [gate_up, qkv, gains],
        [(gate_up.shape, BF16, False), (qkv.shape, BF16, False), (lanes, F32, True)],
        [
            pltpu.VMEM(gains.shape, F32),
            pltpu.VMEM((4, 4) + lanes, F32),
            pltpu.VMEM((3, 4) + lanes, F32),
            pltpu.VMEM((4,) + lanes, F32),
            pltpu.VMEM((3,) + lanes, F32),
        ],
        GROUP_PEERS + FAR_PEERS,
        9,
        64,
        1 << 20,
        (2,),
    )


def per_device(
    inputs, w_query, key_weight, value_weight, w_out, w_gate, w_up, w_down, norm_gains, segments, cotangent
):
    rows, width = inputs.shape
    ways = 8
    teams = 16
    group = QUERY_HEADS // KEY_VALUE_HEADS
    shard = w_query.shape[0]
    hidden_cut = w_down.shape[0]
    hidden_units = teams * hidden_cut
    tokens = rows * ways
    scale = HEAD_SIZE ** (-0.5)

    qkv_send = jnp.concatenate(
        [
            w_query.reshape(shard, ways, -1),
            key_weight.reshape(shard, ways, -1),
            value_weight.reshape(shard, ways, -1),
        ],
        axis=-1,
    ).transpose(1, 0, 2)
    gate_up_send = jnp.stack([w_gate, w_up], axis=1)
    gate_up_send = gate_up_send.reshape(shard, 2, teams, ways, hidden_cut).transpose(3, 0, 1, 2, 4)
    gate_up_send = gate_up_send.reshape(ways, shard, 2 * hidden_units)
    gain_shard = norm_gains.shape[0]
    gains_own = jnp.pad(norm_gains.astype(F32), (0, 128 - gain_shard)).reshape(1, 128)
    x, segment_blocks, gains, w_qkv, gate_up_own, out_rows = first_exchange(
        inputs, segments.reshape(1, rows), gains_own, qkv_send, gate_up_send, w_out
    )
    w_qkv = w_qkv.reshape(width, -1)
    out_rows = out_rows.reshape(-1, width)
    gains = gains[..., :gain_shard].reshape(-1)
    attn_gain = gains[:width]
    mlp_gain = gains[width : 2 * width]
    query_gain = gains[2 * width : 2 * width + HEAD_SIZE]
    key_gain = gains[2 * width + HEAD_SIZE :]

    x = x.reshape(tokens, width).astype(F32)
    segment_blocks = segment_blocks.reshape(ways, rows)
    normed = (x * rms_scale(x) * attn_gain).astype(BF16)
    qkv = mm(normed, w_qkv, ((1,), (0,)))
    cosine, sine, allowed = rotation_tables(segment_blocks)
    query_pre = qkv[:, : group * HEAD_SIZE].reshape(ways, rows, group, HEAD_SIZE)
    key_pre = qkv[:, group * HEAD_SIZE : (group + 1) * HEAD_SIZE].reshape(ways, rows, HEAD_SIZE)
    value = qkv[:, (group + 1) * HEAD_SIZE :].astype(BF16).reshape(ways, rows, HEAD_SIZE)
    query_r = rms_scale(query_pre)
    key_r = rms_scale(key_pre)
    cosine_q, sine_q = cosine[:, :, None, :], sine[:, :, None, :]
    query = rotate(query_pre * query_r * query_gain, cosine_q, sine_q).astype(BF16)
    key = rotate(key_pre * key_r * key_gain, cosine, sine).astype(BF16)
    scores = jnp.einsum("bqgd,bkd->bgqk", query, key, preferred_element_type=F32) * scale
    scores = jnp.where(allowed[:, None], scores, -1e30)
    exponent = jnp.exp(scores - jnp.max(scores, axis=-1, keepdims=True))
    probs_float = exponent / jnp.sum(exponent, axis=-1, keepdims=True)
    probs = probs_float.astype(BF16)
    attended = jnp.einsum("bgqk,bkd->gdbq", probs, value, preferred_element_type=F32).astype(BF16)
    attended = attended.reshape(group, ways, -1, tokens).transpose(1, 0, 2, 3)
    attended = swap_call(2, attended)[0].reshape(-1, tokens)
    out_terms = mm(attended, out_rows, ((0,), (0,))).astype(BF16).reshape(ways, rows, width)
    out_sum, gate_up_rows = sum_and_gather(3, out_terms, gate_up_own, -3)
    gate_up_rows = gate_up_rows.reshape(width, -1)
    hidden = inputs.astype(F32) + out_sum
    hidden_r = rms_scale(hidden)
    normed_two_own = (hidden * hidden_r * mlp_gain).astype(BF16)
    normed_two, dy, down_rows = gather_both(4, [normed_two_own, cotangent], w_down, -1)
    normed_two, dy = normed_two.reshape(tokens, width), dy.reshape(tokens, width)
    down_rows = down_rows.reshape(-1, width)
    gate_up = mm(normed_two, gate_up_rows, ((1,), (0,)))
    gate, up = gate_up[:, :hidden_units], gate_up[:, hidden_units:]
    s = 1.0 / (1.0 + jnp.exp(-gate))
    silu = gate * s
    active = (silu * up).astype(BF16)
    out_partial = mm(active, down_rows, ((1,), (0,))).astype(BF16)
    d_active = mm(dy, down_rows, ((1,), (1,)))
    d_gate = (d_active * up * (s * (1.0 + gate * (1.0 - s)))).astype(BF16)
    d_up = (d_active * silu).astype(BF16)
    d_gate_up = jnp.concatenate([d_gate, d_up], axis=1)
    grad_down = mm(active, dy, ((0,), (0,)))
    grad_gate_up = mm(normed_two, d_gate_up, ((0,), (0,)))
    d_normed_two_terms = mm(d_gate_up, gate_up_rows, ((1,), (1,))).astype(BF16)
    d_normed_two, grad_w_down = sum_both(
        5,
        [d_normed_two_terms.reshape(ways, rows, width)],
        [grad_down.astype(BF16).reshape(4, 4, hidden_cut, width)],
        [-1],
    )
    d_hidden = cotangent.astype(F32) + rms_backward(hidden, hidden_r, d_normed_two * mlp_gain)
    d_mlp_gain = jnp.sum(d_normed_two * hidden * hidden_r, axis=0)

    out_sum, grad_gate_up, d_hidden_low = sum_both(
        6,
        [out_partial.reshape(ways, rows, width)],
        [grad_gate_up.astype(BF16).reshape(4, 4, ways, shard, -1)],
        [-3],
        d_hidden.astype(BF16),
    )
    output = (hidden + out_sum).astype(BF16)
    d_hidden_low = d_hidden_low.reshape(tokens, width)
    grad_out = mm(attended, d_hidden_low, ((1,), (0,)))
    d_attended = mm(out_rows, d_hidden_low, ((1,), (1,))).astype(BF16)
    d_attended = swap_call(7, d_attended.reshape(ways, group, -1, tokens))[0]
    d_attended = d_attended.transpose(1, 0, 2, 3).reshape(group, HEAD_SIZE, ways, rows)
    d_probs = jnp.einsum("gdbq,bkd->bgqk", d_attended, value, preferred_element_type=F32)
    d_value = jnp.einsum("bgqk,gdbq->bkd", probs, d_attended, preferred_element_type=F32).astype(BF16)
    d_scores = probs_float * (d_probs - jnp.sum(probs_float * d_probs, axis=-1, keepdims=True))
    d_scores = d_scores.astype(BF16)
    d_query = jnp.einsum("bgqk,bkd->bqgd", d_scores, key, preferred_element_type=F32) * scale
    d_key = jnp.einsum("bgqk,bqgd->bkd", d_scores, query, preferred_element_type=F32) * scale
    d_query = rotate_back(d_query, cosine_q, sine_q)
    d_key = rotate_back(d_key, cosine, sine)
    d_query_gain = jnp.sum(d_query * query_pre * query_r, axis=(0, 1, 2))
    d_key_gain = jnp.sum(d_key * key_pre * key_r, axis=(0, 1))
    d_query = rms_backward(query_pre, query_r, d_query * query_gain).astype(BF16)
    d_key = rms_backward(key_pre, key_r, d_key * key_gain).astype(BF16)
    d_qkv = jnp.concatenate(
        [d_query.reshape(tokens, -1), d_key.reshape(tokens, -1), d_value.reshape(tokens, -1)], axis=1
    )
    grad_qkv = mm(normed, d_qkv, ((0,), (0,)))
    d_normed, grad_qkv, grad_w_out = sum_both(
        8,
        [mm(d_qkv, w_qkv, ((1,), (1,))).astype(BF16).reshape(ways, rows, width)],
        [
            grad_qkv.astype(BF16).reshape(4, 4, ways, shard, -1),
            grad_out.astype(BF16).reshape(4, 4, shard, width),
        ],
        [-3, -1],
    )
    own = inputs.astype(F32)
    own_r = rms_scale(own)
    grad_inputs = d_hidden + rms_backward(own, own_r, d_normed * attn_gain)
    d_attn_gain = jnp.sum(d_normed * own * own_r, axis=0)
    gain_terms = jnp.concatenate([d_attn_gain, d_mlp_gain, d_query_gain, d_key_gain])
    gain_terms = gain_terms.reshape(4, 4, ways, gain_shard).transpose(2, 0, 1, 3)
    gain_terms = jnp.pad(gain_terms, ((0, 0),) * 3 + ((0, 128 - gain_shard),))
    grad_gate_up, grad_qkv, grad_gains = last_exchange(
        grad_gate_up, grad_qkv, gain_terms.reshape(ways, 4, 4, 1, 128)
    )
    grad_gains = grad_gains[0, :gain_shard]
    grad_gate_up = grad_gate_up.reshape(ways, shard, 2, teams, hidden_cut).transpose(2, 1, 3, 0, 4)
    grad_gate_up = grad_gate_up.reshape(2, shard, -1).astype(F32)
    grad_qkv = grad_qkv.transpose(1, 0, 2).astype(F32)
    grad_w_query = grad_qkv[:, :, : group * HEAD_SIZE].reshape(shard, -1)
    grad_w_key = grad_qkv[:, :, group * HEAD_SIZE : (group + 1) * HEAD_SIZE].reshape(shard, -1)
    grad_w_value = grad_qkv[:, :, (group + 1) * HEAD_SIZE :].reshape(shard, -1)
    grad_w_down = grad_w_down.astype(F32)
    grad_w_out = grad_w_out.astype(F32)
    return (
        output,
        grad_inputs,
        grad_w_query,
        grad_w_key,
        grad_w_value,
        grad_w_out,
        grad_gate_up[0],
        grad_gate_up[1],
        grad_w_down,
        grad_gains,
    )


def solution(mesh):
    cube = Mesh(mesh.devices.reshape(4, 4, 4, 2), ("y", "z", "x", "c"))
    every = ("y", "z", "x", "c")
    matrix, vector = P(every, None), P(every)
    return jax.shard_map(
        per_device,
        mesh=cube,
        in_specs=(matrix,) * 8 + (vector, vector, matrix),
        out_specs=(matrix,) * 9 + (vector,),
        check_vma=False,
    )
```
